256 devices in a mesh: sub: 32 (over x, y, core), fac: 8 (over z).
Axes of the slice: x: 4, y: 4, z: 8, core: 2. Of those that a mesh axis runs over, the one named last changes fastest.
Arguments:
- subgrids: bfloat16 [2, 256, 512, 512], P(None, 'sub', 'fac'), may hold values from -6 to 6
- sub_offsets: int32 [256, 2], replicated, may hold values from 0 to 127, as said below
- coverage: int32 [256], replicated, may hold values from 0 to 1, as said below
- facet_offsets: int32 [2, 4], replicated, may hold values from 0 to 1023
Outputs:
- facet_strips: float32 [2, 2, 16, 256, 16384], P(None, None, 'fac', 'sub')
The draws below stay inside these ranges and needn't reach their ends.
Inputs may be any that keep to these rules, and one draw needn't show every extreme that they name: `sub_offsets`: column in the first entry (0 to 1), position in the second; within a column no position repeats. `coverage`: among the 8 slots of one index of sub at least one and at most 4 are present; on some index exactly 4.
All inputs are finite; a program needn't handle non-finite values.
Results may differ from the reference program's by a relative error of at most 0.0045.
Values may be sent and summed in bfloat16 or wider, within the bound.
A program may use at most 128 MiB of HBM per device.

```python
import math
import jax
import jax.numpy as jnp
from jax import lax

XA = 512
XMYN = 256
VGRID = 128
FROWS = 4
COLS = 2
SLOT_DEV = 8
XM = 1024
YN = 16384
FACETS = 16
MOST = 4
SLOTS = 256


def subgrid_layout(key):
    owners = SLOTS // SLOT_DEV
    places = jax.random.permutation(jax.random.fold_in(key, 101), COLS * VGRID)[:SLOTS].astype(jnp.int32)
    column = places // VGRID
    position = places % VGRID
    counts = jax.random.randint(jax.random.fold_in(key, 102), (owners,), 1, MOST + 1)
    busiest = jax.random.randint(jax.random.fold_in(key, 103), (), 0, owners)
    counts = jnp.where(jnp.arange(owners) == busiest, MOST, counts)
    distance = jnp.abs(2 * position - (VGRID - 1))
    ranking = (distance * SLOTS + jnp.arange(SLOTS, dtype=jnp.int32)).reshape(owners, SLOT_DEV)
    placing = jnp.argsort(jnp.argsort(ranking, axis=1), axis=1)
    present = (placing < counts[:, None]).reshape(-1).astype(jnp.int32)
    return (column, position, present)


def draw_sub_offsets(key, part):
    column, position, present = subgrid_layout(key)
    return jnp.stack([column, position], axis=1).astype(jnp.int32)


def draw_coverage(key, part):
    column, position, present = subgrid_layout(key)
    return present


def set_ends(array, key, low, top_value):
    longest = array.shape.index(max(array.shape))
    spots = []
    for shift in (0, 1):
        where = [jax.random.randint(jax.random.fold_in(key, axis), (), 0, length) for axis, length in enumerate(array.shape)]
        where[longest] = (where[longest] + shift) % array.shape[longest]
        spots.append(tuple(where))
    return array.at[spots[0]].set(low).at[spots[1]].set(top_value)


def steps_of(own_key, extent, pieces, least, top_value):
    def one(axis_at, shards_of):
        steps = jax.random.uniform(jax.random.fold_in(jax.random.fold_in(own_key, 6), axis_at), (shards_of,), jnp.float32, least / len(pieces), top_value / len(pieces))
        return jnp.repeat(jnp.exp(steps), extent[axis_at] // shards_of).reshape((-1,) + (1,) * (len(extent) - axis_at - 1))

    gain = one(*pieces[0])
    for cut in pieces[1:]:
        gain = gain * one(*cut)
    return gain


def gaussian(stream_key, dims, width, reach, shards=(), kind=jnp.bfloat16):
    drawn = jax.random.normal(stream_key, dims, jnp.float32) * width
    if len(shards) > 0:
        drawn = steps_of(stream_key, dims, shards, -0.22, 0.18) * drawn
    return jnp.clip(drawn, min=-reach, max=reach).astype(kind)


def setup_inputs(seed: int = 0) -> dict:
    keys = jax.random.split(jax.random.key(seed), 5)
    subgrids = gaussian(keys[0], (2, SLOTS, XA, XA), 1.0, 6.0, ((1, 32), (2, 8)))
    sub_offsets = draw_sub_offsets(jax.random.fold_in(keys[4], 71), 0)
    coverage = draw_coverage(jax.random.fold_in(keys[4], 71), 0)
    facet_offsets = set_ends(jax.random.randint(keys[3], (2, FROWS), 0, XM), jax.random.fold_in(keys[3], 1), 0, XM - 1).astype(jnp.int32)
    return dict(subgrids=subgrids, sub_offsets=sub_offsets, coverage=coverage, facet_offsets=facet_offsets)


TAPER = 0.6

def build_tables(centres):
    middle = XMYN // 2
    samples = jnp.arange(XMYN, dtype=jnp.int32)
    pixels = jnp.arange(XA, dtype=jnp.int32)
    folded = jnp.mod((samples[:, None] - middle) * (samples[None, :] - middle), XMYN)
    kernel_angles = 2.0 * math.pi / XMYN * folded.astype(jnp.float32)
    kernel_real = jnp.cos(kernel_angles)
    kernel_imag = -jnp.sin(kernel_angles)
    taper = jnp.exp(-0.5 * ((samples.astype(jnp.float32) - middle) / (TAPER * middle)) ** 2)
    exact = lax.Precision.HIGHEST
    factor = 1.0 / math.sqrt(XMYN * XA)

    def one_table(centre):
        phases = jnp.mod((centre + samples[:, None] - middle) * (pixels[None, :] - XA // 2), XM)
        wave_angles = 2.0 * math.pi / XM * phases.astype(jnp.float32)
        wave_real = taper[:, None] * jnp.cos(wave_angles)
        wave_imag = taper[:, None] * jnp.sin(wave_angles)
        table_real = jnp.dot(kernel_real, wave_real, precision=exact, preferred_element_type=jnp.float32) - jnp.dot(kernel_imag, wave_imag, precision=exact, preferred_element_type=jnp.float32)
        table_imag = jnp.dot(kernel_real, wave_imag, precision=exact, preferred_element_type=jnp.float32) + jnp.dot(kernel_imag, wave_real, precision=exact, preferred_element_type=jnp.float32)
        return (jnp.stack([table_real, table_imag]) * factor).astype(jnp.bfloat16)
    return lax.map(one_table, centres)

def reference(subgrids, sub_offsets, coverage, facet_offsets):
    row_tables = build_tables(facet_offsets[0]).astype(jnp.float32)
    col_tables = build_tables(facet_offsets[1]).astype(jnp.float32)
    block_width = XMYN // 2
    strips = jnp.zeros((2, COLS, FACETS, XMYN, YN), jnp.float32)

    def one_slot(slot_index, strips):
        subgrid = subgrids[:, slot_index].astype(jnp.float32)
        real_u = jnp.einsum('fjx,xy->fjy', row_tables[:, 0], subgrid[0]) - jnp.einsum('fjx,xy->fjy', row_tables[:, 1], subgrid[1])
        imag_u = jnp.einsum('fjx,xy->fjy', row_tables[:, 0], subgrid[1]) + jnp.einsum('fjx,xy->fjy', row_tables[:, 1], subgrid[0])
        halfway = jnp.stack([real_u, imag_u]).astype(jnp.bfloat16)
        halfway = lax.optimization_barrier(halfway).astype(jnp.float32)
        real_v = jnp.einsum('ujy,vky->uvjk', halfway[0], col_tables[:, 0]) - jnp.einsum('ujy,vky->uvjk', halfway[1], col_tables[:, 1])
        imag_v = jnp.einsum('ujy,vky->uvjk', halfway[0], col_tables[:, 1]) + jnp.einsum('ujy,vky->uvjk', halfway[1], col_tables[:, 0])
        weight = coverage[slot_index].astype(jnp.float32)
        contrib = jnp.stack([real_v, imag_v]).reshape(2, FACETS, XMYN, XMYN) * weight
        column = sub_offsets[slot_index, 0].astype(jnp.int32)
        position = sub_offsets[slot_index, 1].astype(jnp.int32)
        lower = (jnp.mod(position - 1, VGRID) * block_width).astype(jnp.int32)
        upper = (position * block_width).astype(jnp.int32)
        anchor = jnp.zeros((), jnp.int32)
        for offset, segment in ((lower, contrib[..., :block_width]), (upper, contrib[..., block_width:])):
            corner = (anchor, column, anchor, anchor, offset)
            region = lax.dynamic_slice(strips, corner, (2, 1, FACETS, XMYN, block_width))
            strips = lax.dynamic_update_slice(strips, region + segment[:, None], corner)
        return strips
    return lax.fori_loop(0, SLOTS, one_slot, strips)
```

```python
import functools
import math

import jax
import jax.numpy as jnp
import numpy as np
from jax import lax
from jax.experimental import pallas as pl
from jax.experimental.pallas import tpu as pltpu
from jax.sharding import PartitionSpec as P

XA = 512
XMYN = 256
VGRID = 128
FROWS = 4
COLS = 2
XM = 1024
YN = 16384
SLOT_DEV = 8
MOST = 4
OWNERS = 32
FAC = 8
XB = XA // FAC
ROWS = XMYN // OWNERS
TAPER = 0.6
SECTIONS = 4

MESH = pl.DeviceIdType.MESH

HALF = XA // 2

CHUNKS = ((0, 0, 1), (0, 1, 1), (1, 0, 1), (1, 1, 1), (2, 0, 1), (2, 1, 1), (3, 0, 1), (3, 1, 1))

SCHEDULE = ((0, 1), (1, 1), (2, 1), 'T', (3, 1), (0, 2), (1, 2), (2, 2), (3, 2), (0, 3), (1, 3), (2, 3), (4, 1), (0, 4), (1, 4), (5, 1), (3, 3), (2, 4), 'F0', 'F1', (4, 2), (3, 4), (6, 1), (5, 2), 'F2', (4, 3), (7, 1), 'F3', (5, 3), (6, 2), 'G0', (4, 4), (7, 2), 'G1', (5, 4), (6, 3), 'F4', (7, 3), 'G2', 'F5', (6, 4), (7, 4), 'G3', 'F6', 'F7', 'G4', 'G5', 'G6', 'G7')


def base_table():
    h = XMYN // 2
    k = np.arange(XMYN) - h
    x = np.arange(XA) - XA // 2
    kernel = np.exp(-2j * np.pi / XMYN * np.mod(k[:, None] * k[None, :], XMYN))
    taper = np.exp(-0.5 * (k / (TAPER * h)) ** 2)
    wave = np.exp(2j * np.pi / XM * np.mod(k[:, None] * x[None, :], XM))
    return kernel @ (taper[:, None] * wave) / math.sqrt(XMYN * XA)


def constants():
    table = base_table()
    real = table.real.astype(np.float32)
    imag = table.imag.astype(np.float32)

    return np.stack([real, imag])


def phases(centre, pixel):
    index = (centre * (pixel - XA // 2)) & (XM - 1)
    angle = (2.0 * math.pi / XM) * index.astype(jnp.float32)
    return jnp.cos(angle), jnp.sin(angle)


def exchange_kernel(
    cov_ref,
    centre_ref,
    cov_hbm,
    off_hbm,
    sub_hbm,
    base_hbm,
    out_hbm,
    where_ref,
    cov_vec,
    off_vec,
    sub_ref,
    seg,
    row_table,
    col_table,
    half,
    recv,
    base,
    stage,
    ring_send,
    ring_recv,
    swap_send,
    swap_recv,
    load_sem,
    out_sem,
):
    s = lax.axis_index("sub")
    f = lax.axis_index("fac")
    right = lax.rem(f + 1, FAC)
    left = lax.rem(f + FAC - 1, FAC)

    load_sub = pltpu.make_async_copy(sub_hbm, sub_ref, load_sem.at[0])
    load_base = pltpu.make_async_copy(base_hbm, base, load_sem.at[1])
    load_cov = pltpu.make_async_copy(cov_hbm, cov_vec, load_sem.at[2])
    load_off = pltpu.make_async_copy(off_hbm, off_vec, load_sem.at[3])
    for load in (load_sub, load_base, load_cov, load_off):
        load.start()

    barrier = pltpu.get_barrier_semaphore()
    for neighbour in (left, right):
        pl.semaphore_signal(barrier, inc=1, device_id=(s, neighbour), device_id_type=MESH)

    @pl.loop(1, OWNERS)
    def _(d):
        pl.semaphore_signal(
            barrier, inc=1, device_id=(lax.rem(s + d, OWNERS), f), device_id_type=MESH
        )

    chosen = [jnp.int32(0)] * MOST
    count = jnp.int32(0)
    for i in range(SLOT_DEV):
        here = cov_ref[s * SLOT_DEV + i] > 0
        chosen = [
            jnp.where(jnp.logical_and(here, count == q), i, chosen[q]) for q in range(MOST)
        ]
        count = count + here.astype(jnp.int32)
    load_sub.wait()
    for t in range(MOST):
        for ri in range(2):
            block = sub_ref[ri, chosen[t]]
            for h in range(2):
                seg[t, h, ri, f] = block[:, h * HALF : (h + 1) * HALF]

    pl.semaphore_wait(barrier, OWNERS + 1)

    def ring_ref(way, c, step, origin):
        t, h, n = CHUNKS[c]
        part = seg.at[t, pl.ds(h, n)]
        return part.at[:, :, origin] if step < 4 else part.at[:, way, origin]

    def piece(way, c, step):
        if way == 0:
            origin, target = lax.rem(f + FAC - (step - 1), FAC), right
        else:
            origin, target = lax.rem(f + step - 1, FAC), left
        ref = ring_ref(way, c, step, origin)
        return pltpu.make_async_remote_copy(
            src_ref=ref,
            dst_ref=ref,
            send_sem=ring_send.at[way, c, step - 1],
            recv_sem=ring_recv.at[way, c, step - 1],
            device_id=(s, target),
            device_id_type=MESH,
        )

    def arrived(way, c, step):
        if way == 0:
            origin = lax.rem(f + FAC - step, FAC)
        else:
            origin = lax.rem(f + step, FAC)
        ref = ring_ref(way, c, step, origin)
        pltpu.make_async_copy(ref, ref, ring_recv.at[way, c, step - 1]).wait()

    def issue(c, step):
        for way in range(2):
            if step > 1:
                arrived(way, c, step - 1)
            piece(way, c, step).start()

    def tables():
        load_base.wait()
        pixel = lax.broadcasted_iota(jnp.int32, (1, XA), 1)

        def centred(centre):
            cosine, sine = phases(centre, pixel)
            return cosine * base[0] - sine * base[1], cosine * base[1] + sine * base[0]

        parts = [part.reshape(OWNERS, ROWS, XA) for part in centred(centre_ref[0, f // 2])]
        for first, part in ((0, parts), (XA, (-parts[1], parts[0]))):
            row_table[:, first : first + XA] = (
                jnp.concatenate(part, axis=1).reshape(2 * XMYN, XA).astype(jnp.bfloat16)
            )
        for v in range(2):
            for ri, part in enumerate(centred(centre_ref[1, lax.rem(f, 2) * 2 + v])):
                first = (v * 2 + ri) * XMYN
                col_table[first : first + XMYN, :] = part.astype(jnp.bfloat16)
        places()

    def places():
        load_cov.wait()
        load_off.wait()
        slots = OWNERS * SLOT_DEV
        here = cov_vec[0:1, :]
        row = lax.broadcasted_iota(jnp.int32, (slots, slots), 0)
        col = lax.broadcasted_iota(jnp.int32, (slots, slots), 1)
        before = jnp.logical_and(row // SLOT_DEV == col // SLOT_DEV, col < row)
        lhs = jnp.broadcast_to(here, (8, slots)).astype(jnp.bfloat16)
        nt = (((1,), (1,)), ((), ()))
        rank = lax.dot_general(
            lhs, before.astype(jnp.bfloat16), nt, preferred_element_type=jnp.float32
        )
        owner = lax.broadcasted_iota(jnp.int32, (8, slots), 1) // SLOT_DEV
        source = lax.rem(owner - s + OWNERS, OWNERS)
        code = (rank * OWNERS + source.astype(jnp.float32) + 1.0) * lhs.astype(jnp.float32)
        target = off_vec[0:1, :] * VGRID + off_vec[1:2, :]
        hit = (row == target).astype(jnp.bfloat16)
        found = lax.dot_general(
            code.astype(jnp.bfloat16), hit, nt, preferred_element_type=jnp.float32
        )
        where_ref[...] = found.astype(jnp.int32)

    def swap_copy(c, d):
        t, h, n = CHUNKS[c]
        target = lax.rem(s + d, OWNERS)
        return pltpu.make_async_remote_copy(
            src_ref=half.at[t, pl.ds(h, n), target],
            dst_ref=recv.at[t, pl.ds(h, n), OWNERS - d],
            send_sem=swap_send.at[c],
            recv_sem=swap_recv.at[c],
            device_id=(target, f),
            device_id_type=MESH,
        )

    def row_pass(c):
        t, first, n = CHUNKS[c]
        for way in range(2):
            arrived(way, c, 4)
        for h in range(first, first + n):
            block = seg[t, h].reshape(2 * XA, HALF)
            product = jnp.dot(row_table[...], block, preferred_element_type=jnp.float32)
            half[t, h] = product.astype(jnp.bfloat16).reshape(OWNERS, 2 * ROWS, HALF)

        @pl.loop(1, OWNERS)
        def _(d):
            swap_copy(c, d).start()

        for h in range(first, first + n):
            recv[t, h, 0] = half[t, h, s]

    def out_copy(t):
        return pltpu.make_async_copy(stage.at[t % 2], out_hbm.at[t], out_sem.at[t])

    def column_pass(c):
        t, first, n = CHUNKS[c]
        whole = recv.at[t, pl.ds(first, n), pl.ds(1, OWNERS - 1)]
        pltpu.make_async_copy(whole, whole, swap_recv.at[c]).wait()
        if t >= 2 and first == 0:
            out_copy(t - 2).wait()
        for v in range(2):
            product = []
            for ri in range(2):
                rows = slice((v * 2 + ri) * XMYN, (v * 2 + ri + 1) * XMYN)
                total = None
                for h in range(first, first + n):
                    term = lax.dot_general(
                        recv[t, h].reshape(OWNERS * 2 * ROWS, HALF),
                        col_table[rows, h * HALF : (h + 1) * HALF],
                        (((1,), (1,)), ((), ())),
                        preferred_element_type=jnp.float32,
                    )
                    total = term if total is None else total + term
                product.append(total.reshape(OWNERS, 2, ROWS, XMYN))
            real = product[0][:, 0] - product[1][:, 1]
            imag = product[1][:, 0] + product[0][:, 1]
            for ri, value in enumerate((real, imag)):
                for part in range(2):
                    tile = value[:, :, part * VGRID : (part + 1) * VGRID]
                    k = (ri * 2 + v) * 2 + part
                    if first > 0:
                        tile = tile + stage[t % 2, :, k]
                    stage[t % 2, :, k] = tile
        if first + n == 2:
            out_copy(t).start()

    for entry in SCHEDULE:
        if entry == "T":
            tables()
        elif isinstance(entry, tuple):
            issue(*entry)
        elif entry[0] == "F":
            row_pass(int(entry[1:]))
        else:
            column_pass(int(entry[1:]))

    for c, (t, first, n) in enumerate(CHUNKS):
        for step in range(1, 5):
            for way in range(2):
                piece(way, c, step).wait_send()
        whole = half.at[t, pl.ds(first, n), pl.ds(1, OWNERS - 1)]
        pltpu.make_async_copy(whole, whole, swap_send.at[c]).wait()
    out_copy(MOST - 2).wait()
    out_copy(MOST - 1).wait()


def place_kernel(where_ref, pieces_ref, out_hbm, strips, out_sem):
    stores = []
    span = VGRID // SECTIONS
    for c in range(COLS):

        def at(p):
            code = where_ref[0, c * VGRID + (p & (VGRID - 1))]
            return jnp.maximum(code - 1, 0), (code > 0).astype(jnp.float32)

        def body(p, here, at=at, c=c):
            after = at(p + 1)
            lanes = pl.ds(pl.multiple_of(p * VGRID, VGRID), VGRID)
            for k in range(4):
                strips[k, c, :, lanes] = (
                    here[1] * pieces_ref[here[0], 2 * k + 1]
                    + after[1] * pieces_ref[after[0], 2 * k]
                )
            return after

        here = at(0)
        for q in range(SECTIONS):
            here = lax.fori_loop(q * span, (q + 1) * span, body, here, unroll=8)
            lanes = pl.ds(q * span * VGRID, span * VGRID)
            for k in range(4):
                store = pltpu.make_async_copy(
                    strips.at[k, c, :, lanes],
                    out_hbm.at[k // 2, c, k % 2, :, lanes],
                    out_sem.at[k, c, q],
                )
                store.start()
                stores.append(store)
    for store in stores:
        store.wait()


def local(subgrids, sub_offsets, coverage, facet_offsets):
    base = constants()
    smem = pl.BlockSpec(memory_space=pltpu.SMEM)
    vmem = pl.BlockSpec(memory_space=pltpu.VMEM)
    hbm = pl.BlockSpec(memory_space=pltpu.HBM)
    anywhere = pl.BlockSpec(memory_space=pl.ANY)
    bf16, f32 = jnp.bfloat16, jnp.float32
    dma = pltpu.SemaphoreType.DMA
    hb = lambda x: pltpu.with_memory_space_constraint(x, pltpu.HBM)
    slots = OWNERS * SLOT_DEV
    chunks = len(CHUNKS)
    pieces, where = pl.pallas_call(
        exchange_kernel,
        out_shape=[
            jax.ShapeDtypeStruct((MOST, OWNERS, 8, ROWS, VGRID), f32),
            jax.ShapeDtypeStruct((8, slots), jnp.int32),
        ],
        in_specs=[smem, smem, hbm, hbm, hbm, hbm],
        out_specs=[anywhere, vmem],
        scratch_shapes=[
            pltpu.VMEM((1, slots), jnp.int32),
            pltpu.VMEM((2, slots), jnp.int32),
            pltpu.VMEM((2, SLOT_DEV, XB, XA), bf16),
            pltpu.VMEM((MOST, 2, 2, FAC, XB, HALF), bf16),
            pltpu.VMEM((2 * XMYN, 2 * XA), bf16),
            pltpu.VMEM((4 * XMYN, XA), bf16),
            pltpu.VMEM((MOST, 2, OWNERS, 2 * ROWS, HALF), bf16),
            pltpu.VMEM((MOST, 2, OWNERS, 2 * ROWS, HALF), bf16),
            pltpu.VMEM((2, XMYN, XA), f32),
            pltpu.VMEM((2, OWNERS, 8, ROWS, VGRID), f32),
            dma((2, chunks, 4)),
            dma((2, chunks, 4)),
            dma((chunks,)),
            dma((chunks,)),
            dma((4,)),
            dma((MOST,)),
        ],
        compiler_params=pltpu.CompilerParams(
            collective_id=0, has_side_effects=True, vmem_limit_bytes=40 * 2**20
        ),
        name="exchange",
    )(
        hb(coverage),
        hb(facet_offsets),
        hb(coverage.reshape(1, slots)),
        hb(sub_offsets.T),
        hb(subgrids),
        hb(jnp.asarray(base)),
    )
    return pl.pallas_call(
        place_kernel,
        out_shape=jax.ShapeDtypeStruct((2, COLS, 2, ROWS, YN), f32),
        in_specs=[smem, vmem],
        out_specs=anywhere,
        scratch_shapes=[
            pltpu.VMEM((4, COLS, ROWS, YN), f32),
            dma((4, COLS, SECTIONS)),
        ],
        compiler_params=pltpu.CompilerParams(vmem_limit_bytes=40 * 2**20),
        name="place",
    )(where, pieces.reshape(MOST * OWNERS, 8, ROWS, VGRID))


def solution(mesh):
    placed = (P(None, "sub", "fac", None), P(), P(), P())
    return jax.shard_map(
        local,
        mesh=mesh,
        in_specs=placed,
        out_specs=P(None, None, "fac", "sub", None),
        check_vma=False,
    )
```

```python
import functools
import math

import jax
import jax.numpy as jnp
import numpy as np
from jax import lax
from jax.experimental import pallas as pl
from jax.experimental.pallas import tpu as pltpu
from jax.sharding import PartitionSpec as P

XA = 512
XMYN = 256
VGRID = 128
FROWS = 4
COLS = 2
XM = 1024
YN = 16384
SLOT_DEV = 8
MOST = 4
OWNERS = 32
FAC = 8
XB = XA // FAC
ROWS = XMYN // OWNERS
TAPER = 0.6
SECTIONS = 8

MESH = pl.DeviceIdType.MESH

HALF = XA // 2

CHUNKS = ((0, 0, 1), (0, 1, 1), (1, 0, 1), (1, 1, 1), (2, 0, 1), (2, 1, 1), (3, 0, 1), (3, 1, 1))

SCHEDULE = ((0, 1), (1, 1), (2, 1), 'T', (3, 1), (0, 2), (1, 2), (2, 2), (3, 2), (0, 3), (1, 3), (2, 3), (4, 1), (0, 4), (1, 4), (5, 1), (3, 3), (2, 4), 'F0', (4, 2), 'F1', (3, 4), (6, 1), (5, 2), 'F2', (4, 3), (7, 1), (5, 3), 'F3', (6, 2), (4, 4), (7, 2), 'G0', (5, 4), (6, 3), 'G1', 'F4', (7, 3), 'G2', 'F5', (6, 4), (7, 4), 'G3', 'F6', 'F7', 'G4', 'G5', 'G6', 'G7')


def base_table():
    h = XMYN // 2
    k = np.arange(XMYN) - h
    x = np.arange(XA) - XA // 2
    kernel = np.exp(-2j * np.pi / XMYN * np.mod(k[:, None] * k[None, :], XMYN))
    taper = np.exp(-0.5 * (k / (TAPER * h)) ** 2)
    wave = np.exp(2j * np.pi / XM * np.mod(k[:, None] * x[None, :], XM))
    return kernel @ (taper[:, None] * wave) / math.sqrt(XMYN * XA)


def constants():
    table = base_table()
    real = table.real.astype(np.float32)
    imag = table.imag.astype(np.float32)

    return np.stack([real, imag])


def phases(centre, pixel):
    index = (centre * (pixel - XA // 2)) & (XM - 1)
    angle = (2.0 * math.pi / XM) * index.astype(jnp.float32)
    return jnp.cos(angle), jnp.sin(angle)


def shifted(index, by, sign=1):
    x = ((index >> 3) + sign * (by >> 3)) & 3
    y = ((index >> 1 & 3) + sign * (by >> 1 & 3)) & 3
    return x * 8 + y * 2 + ((index ^ by) & 1)


def hops(by):
    x, y = by >> 3, by >> 1 & 3
    return min(x, 4 - x) + min(y, 4 - y)


FARTHEST = sorted(range(1, OWNERS), key=lambda by: -hops(by))


def exchange_kernel(
    cov_ref,
    centre_ref,
    cov_hbm,
    off_hbm,
    sub_hbm,
    base_hbm,
    pieces_ref,
    where_ref,
    cov_vec,
    off_vec,
    sub_ref,
    seg,
    row_table,
    col_table,
    half,
    recv,
    base,
    ring_send,
    ring_recv,
    swap_send,
    swap_recv,
    load_sem,
):
    s = lax.axis_index("sub")
    f = lax.axis_index("fac")
    right = lax.rem(f + 1, FAC)
    left = lax.rem(f + FAC - 1, FAC)

    load_sub = pltpu.make_async_copy(sub_hbm, sub_ref, load_sem.at[0])
    load_base = pltpu.make_async_copy(base_hbm, base, load_sem.at[1])
    load_cov = pltpu.make_async_copy(cov_hbm, cov_vec, load_sem.at[2])
    load_off = pltpu.make_async_copy(off_hbm, off_vec, load_sem.at[3])
    for load in (load_sub, load_base, load_cov, load_off):
        load.start()

    barrier = pltpu.get_barrier_semaphore()
    for neighbour in (left, right):
        pl.semaphore_signal(barrier, inc=1, device_id=(s, neighbour), device_id_type=MESH)

    for d in range(1, OWNERS):
        pl.semaphore_signal(
            barrier, inc=1, device_id=(lax.rem(s + d, OWNERS), f), device_id_type=MESH
        )

    chosen = [jnp.int32(0)] * MOST
    count = jnp.int32(0)
    for i in range(SLOT_DEV):
        here = cov_ref[s * SLOT_DEV + i] > 0
        chosen = [
            jnp.where(jnp.logical_and(here, count == q), i, chosen[q]) for q in range(MOST)
        ]
        count = count + here.astype(jnp.int32)
    load_sub.wait()
    for t in range(MOST):
        for ri in range(2):
            block = sub_ref[ri, chosen[t]]
            for h in range(2):
                seg[t, h, ri, f] = block[:, h * HALF : (h + 1) * HALF]

    pl.semaphore_wait(barrier, OWNERS + 1)

    def ring_ref(way, c, step, origin):
        t, h, n = CHUNKS[c]
        part = seg.at[t, pl.ds(h, n)]
        return part.at[:, :, origin] if step < 4 else part.at[:, way, origin]

    def piece(way, c, step):
        if way == 0:
            origin, target = lax.rem(f + FAC - (step - 1), FAC), right
        else:
            origin, target = lax.rem(f + step - 1, FAC), left
        ref = ring_ref(way, c, step, origin)
        return pltpu.make_async_remote_copy(
            src_ref=ref,
            dst_ref=ref,
            send_sem=ring_send.at[way, c, step - 1],
            recv_sem=ring_recv.at[way, c, step - 1],
            device_id=(s, target),
            device_id_type=MESH,
        )

    def arrived(way, c, step):
        if way == 0:
            origin = lax.rem(f + FAC - step, FAC)
        else:
            origin = lax.rem(f + step, FAC)
        ref = ring_ref(way, c, step, origin)
        pltpu.make_async_copy(ref, ref, ring_recv.at[way, c, step - 1]).wait()

    def issue(c, step):
        for way in range(2):
            if step > 1:
                arrived(way, c, step - 1)
            piece(way, c, step).start()

    def tables():
        load_base.wait()
        pixel = lax.broadcasted_iota(jnp.int32, (1, XA), 1)

        def centred(centre):
            cosine, sine = phases(centre, pixel)
            return cosine * base[0] - sine * base[1], cosine * base[1] + sine * base[0]

        parts = [part.reshape(OWNERS, ROWS, XA) for part in centred(centre_ref[0, f // 2])]
        for first, part in ((0, parts), (XA, (-parts[1], parts[0]))):
            row_table[:, first : first + XA] = (
                jnp.concatenate(part, axis=1).reshape(2 * XMYN, XA).astype(jnp.bfloat16)
            )
        for v in range(2):
            for ri, part in enumerate(centred(centre_ref[1, lax.rem(f, 2) * 2 + v])):
                first = (v * 2 + ri) * XMYN
                col_table[first : first + XMYN, :] = part.astype(jnp.bfloat16)
        places()

    def places():
        load_cov.wait()
        load_off.wait()
        slots = OWNERS * SLOT_DEV
        here = cov_vec[0:1, :]
        row = lax.broadcasted_iota(jnp.int32, (slots, slots), 0)
        col = lax.broadcasted_iota(jnp.int32, (slots, slots), 1)
        before = jnp.logical_and(row // SLOT_DEV == col // SLOT_DEV, col < row)
        lhs = jnp.broadcast_to(here, (8, slots)).astype(jnp.bfloat16)
        nt = (((1,), (1,)), ((), ()))
        rank = lax.dot_general(
            lhs, before.astype(jnp.bfloat16), nt, preferred_element_type=jnp.float32
        )
        owner = lax.broadcasted_iota(jnp.int32, (8, slots), 1) // SLOT_DEV
        source = shifted(owner, s, -1)
        code = (rank * OWNERS + source.astype(jnp.float32) + 1.0) * lhs.astype(jnp.float32)
        target = off_vec[0:1, :] * VGRID + off_vec[1:2, :]
        hit = (row == target).astype(jnp.bfloat16)
        found = lax.dot_general(
            code.astype(jnp.bfloat16), hit, nt, preferred_element_type=jnp.float32
        )
        index = found.astype(jnp.int32) - 1
        where_ref[...] = jnp.where(index < 0, MOST * OWNERS, index)
        pieces_ref[MOST * OWNERS] = jnp.zeros((8, ROWS, VGRID), jnp.float32)

    def swap_copy(c, d):
        t, h, n = CHUNKS[c]
        target, back = shifted(s, d), shifted(0, d, -1)
        return pltpu.make_async_remote_copy(
            src_ref=half.at[t, pl.ds(h, n), target],
            dst_ref=recv.at[t, pl.ds(h, n), back],
            send_sem=swap_send.at[c],
            recv_sem=swap_recv.at[c],
            device_id=(target, f),
            device_id_type=MESH,
        )

    def row_pass(c):
        t, first, n = CHUNKS[c]
        for way in range(2):
            arrived(way, c, 4)
        for h in range(first, first + n):
            block = seg[t, h].reshape(2 * XA, HALF)
            product = jnp.dot(row_table[...], block, preferred_element_type=jnp.float32)
            half[t, h] = product.astype(jnp.bfloat16).reshape(OWNERS, 2 * ROWS, HALF)

        for d in FARTHEST:
            swap_copy(c, d).start()

        for h in range(first, first + n):
            recv[t, h, 0] = half[t, h, s]

    def column_pass(c):
        t, first, n = CHUNKS[c]
        whole = recv.at[t, pl.ds(first, n), pl.ds(1, OWNERS - 1)]
        pltpu.make_async_copy(whole, whole, swap_recv.at[c]).wait()
        for v in range(2):
            product = []
            for ri in range(2):
                rows = slice((v * 2 + ri) * XMYN, (v * 2 + ri + 1) * XMYN)
                total = None
                for h in range(first, first + n):
                    term = lax.dot_general(
                        recv[t, h].reshape(OWNERS * 2 * ROWS, HALF),
                        col_table[rows, h * HALF : (h + 1) * HALF],
                        (((1,), (1,)), ((), ())),
                        preferred_element_type=jnp.float32,
                    )
                    total = term if total is None else total + term
                product.append(total.reshape(OWNERS, 2, ROWS, XMYN))
            real = product[0][:, 0] - product[1][:, 1]
            imag = product[1][:, 0] + product[0][:, 1]
            for ri, value in enumerate((real, imag)):
                for part in range(2):
                    tile = value[:, :, part * VGRID : (part + 1) * VGRID]
                    k = (ri * 2 + v) * 2 + part
                    if first > 0:
                        tile = tile + pieces_ref[t * OWNERS : (t + 1) * OWNERS, k]
                    pieces_ref[t * OWNERS : (t + 1) * OWNERS, k] = tile

    for entry in SCHEDULE:
        if entry == "T":
            tables()
        elif isinstance(entry, tuple):
            issue(*entry)
        elif entry[0] == "F":
            row_pass(int(entry[1:]))
        else:
            column_pass(int(entry[1:]))

    for c, (t, first, n) in enumerate(CHUNKS):
        for step in range(1, 5):
            for way in range(2):
                piece(way, c, step).wait_send()
        whole = half.at[t, pl.ds(first, n), pl.ds(1, OWNERS - 1)]
        pltpu.make_async_copy(whole, whole, swap_send.at[c]).wait()


def place_kernel(where_ref, pieces_ref, out_hbm, strips, out_sem):
    stores = []
    span = VGRID // SECTIONS
    for c in range(COLS):

        def at(p, c=c):
            return where_ref[0, c * VGRID + (p & (VGRID - 1))]

        def body(p, here, at=at, c=c):
            after = at(p + 1)
            lanes = pl.ds(pl.multiple_of(p * VGRID, VGRID), VGRID)
            for k in range(4):
                strips[k, c, :, lanes] = (
                    pieces_ref[here, 2 * k + 1] + pieces_ref[after, 2 * k]
                )
            return after

        here = at(0)
        for q in range(SECTIONS):
            here = lax.fori_loop(q * span, (q + 1) * span, body, here, unroll=16)
            lanes = pl.ds(q * span * VGRID, span * VGRID)
            for k in range(4):
                store = pltpu.make_async_copy(
                    strips.at[k, c, :, lanes],
                    out_hbm.at[k // 2, c, k % 2, :, lanes],
                    out_sem.at[k, c, q],
                )
                store.start()
                stores.append(store)
    for store in stores:
        store.wait()


def local(subgrids, sub_offsets, coverage, facet_offsets):
    base = constants()
    smem = pl.BlockSpec(memory_space=pltpu.SMEM)
    vmem = pl.BlockSpec(memory_space=pltpu.VMEM)
    hbm = pl.BlockSpec(memory_space=pltpu.HBM)
    anywhere = pl.BlockSpec(memory_space=pl.ANY)
    bf16, f32 = jnp.bfloat16, jnp.float32
    dma = pltpu.SemaphoreType.DMA
    hb = lambda x: pltpu.with_memory_space_constraint(x, pltpu.HBM)
    slots = OWNERS * SLOT_DEV
    chunks = len(CHUNKS)
    pieces, where = pl.pallas_call(
        exchange_kernel,
        out_shape=[
            jax.ShapeDtypeStruct((MOST * OWNERS + 1, 8, ROWS, VGRID), f32),
            jax.ShapeDtypeStruct((8, slots), jnp.int32),
        ],
        in_specs=[smem, smem, hbm, hbm, hbm, hbm],
        out_specs=[vmem, vmem],
        scratch_shapes=[
            pltpu.VMEM((1, slots), jnp.int32),
            pltpu.VMEM((2, slots), jnp.int32),
            pltpu.VMEM((2, SLOT_DEV, XB, XA), bf16),
            pltpu.VMEM((MOST, 2, 2, FAC, XB, HALF), bf16),
            pltpu.VMEM((2 * XMYN, 2 * XA), bf16),
            pltpu.VMEM((4 * XMYN, XA), bf16),
            pltpu.VMEM((MOST, 2, OWNERS, 2 * ROWS, HALF), bf16),
            pltpu.VMEM((MOST, 2, OWNERS, 2 * ROWS, HALF), bf16),
            pltpu.VMEM((2, XMYN, XA), f32),
            dma((2, chunks, 4)),
            dma((2, chunks, 4)),
            dma((chunks,)),
            dma((chunks,)),
            dma((4,)),
        ],
        compiler_params=pltpu.CompilerParams(
            collective_id=0, has_side_effects=True, vmem_limit_bytes=40 * 2**20
        ),
        name="exchange",
    )(
        hb(coverage),
        hb(facet_offsets),
        hb(coverage.reshape(1, slots)),
        hb(sub_offsets.T),
        hb(subgrids),
        hb(jnp.asarray(base)),
    )
    return pl.pallas_call(
        place_kernel,
        out_shape=jax.ShapeDtypeStruct((2, COLS, 2, ROWS, YN), f32),
        in_specs=[smem, vmem],
        out_specs=anywhere,
        scratch_shapes=[
            pltpu.VMEM((4, COLS, ROWS, YN), f32),
            dma((4, COLS, SECTIONS)),
        ],
        compiler_params=pltpu.CompilerParams(vmem_limit_bytes=40 * 2**20),
        name="place",
    )(where, pieces)


def solution(mesh):
    placed = (P(None, "sub", "fac", None), P(), P(), P())
    return jax.shard_map(
        local,
        mesh=mesh,
        in_specs=placed,
        out_specs=P(None, None, "fac", "sub", None),
        check_vma=False,
    )
```

```python
import functools
import math

import jax
import jax.numpy as jnp
import numpy as np
from jax import lax
from jax.experimental import pallas as pl
from jax.experimental.pallas import tpu as pltpu
from jax.sharding import PartitionSpec as P

XA = 512
XMYN = 256
VGRID = 128
FROWS = 4
COLS = 2
XM = 1024
YN = 16384
SLOT_DEV = 8
MOST = 4
OWNERS = 32
FAC = 8
XB = XA // FAC
ROWS = XMYN // OWNERS
TAPER = 0.6
SECTIONS = 8
GROUP = 8

MESH = pl.DeviceIdType.MESH

HALF = XA // 2

CHUNKS = ((0, 0, 1), (0, 1, 1), (1, 0, 1), (1, 1, 1), (2, 0, 1), (2, 1, 1), (3, 0, 1), (3, 1, 1))

SWAPS = {1: (0, 0, 2), 3: (1, 0, 2), 5: (2, 0, 2), 6: (3, 0, 1), 7: (3, 1, 1)}

SCHEDULE = (
    (0, 1), (1, 1), (2, 1), "T", (3, 1), (0, 2), (1, 2), (2, 2), (3, 2), (0, 3), (1, 3), (2, 3),
    (4, 1), (0, 4), (1, 4), (5, 1), (3, 3), (2, 4), "F0", (4, 2), "F1", (3, 4), (6, 1), (5, 2),
    "F2", (4, 3), (7, 1), (5, 3), "F3", (6, 2), (4, 4), (7, 2), (5, 4), (6, 3), "F4", (7, 3),
    "F5", (6, 4), (7, 4), "F6", "F7", "G1", "G3", "W", "G5",
    "G6", "G7",
)


def base_table():
    h = XMYN // 2
    k = np.arange(XMYN) - h
    x = np.arange(XA) - XA // 2
    kernel = np.exp(-2j * np.pi / XMYN * np.mod(k[:, None] * k[None, :], XMYN))
    taper = np.exp(-0.5 * (k / (TAPER * h)) ** 2)
    wave = np.exp(2j * np.pi / XM * np.mod(k[:, None] * x[None, :], XM))
    return kernel @ (taper[:, None] * wave) / math.sqrt(XMYN * XA)


def constants():
    table = base_table()
    real = table.real.astype(np.float32)
    imag = table.imag.astype(np.float32)

    return np.stack([real, imag])


def phases(centre, pixel):
    index = (centre * (pixel - XA // 2)) & (XM - 1)
    angle = (2.0 * math.pi / XM) * index.astype(jnp.float32)
    return jnp.cos(angle), jnp.sin(angle)


def shifted(index, by, sign=1):
    x = ((index >> 3) + sign * (by >> 3)) & 3
    y = ((index >> 1 & 3) + sign * (by >> 1 & 3)) & 3
    return x * 8 + y * 2 + ((index ^ by) & 1)


def hops(by):
    x, y = by >> 3, by >> 1 & 3
    return min(x, 4 - x) + min(y, 4 - y)


FARTHEST = sorted(range(1, OWNERS), key=lambda by: -hops(by))


def exchange_kernel(
    cov_ref,
    centre_ref,
    cov_hbm,
    off_hbm,
    sub_hbm,
    base_hbm,
    pieces_ref,
    where_ref,
    cov_vec,
    off_vec,
    sub_ref,
    seg,
    row_table,
    col_table,
    half,
    recv,
    base,
    ring_send,
    ring_recv,
    swap_send,
    swap_recv,
    load_sem,
):
    s = lax.axis_index("sub")
    f = lax.axis_index("fac")
    right = lax.rem(f + 1, FAC)
    left = lax.rem(f + FAC - 1, FAC)

    load_sub = pltpu.make_async_copy(sub_hbm, sub_ref, load_sem.at[0])
    load_base = pltpu.make_async_copy(base_hbm, base, load_sem.at[1])
    load_cov = pltpu.make_async_copy(cov_hbm, cov_vec, load_sem.at[2])
    load_off = pltpu.make_async_copy(off_hbm, off_vec, load_sem.at[3])
    for load in (load_sub, load_base, load_cov, load_off):
        load.start()

    barrier = pltpu.get_barrier_semaphore()
    for neighbour in (left, right):
        pl.semaphore_signal(barrier, inc=1, device_id=(s, neighbour), device_id_type=MESH)

    for d in range(1, OWNERS):
        pl.semaphore_signal(
            barrier, inc=1, device_id=(lax.rem(s + d, OWNERS), f), device_id_type=MESH
        )

    chosen = [jnp.int32(0)] * MOST
    count = jnp.int32(0)
    for i in range(SLOT_DEV):
        here = cov_ref[s * SLOT_DEV + i] > 0
        chosen = [
            jnp.where(jnp.logical_and(here, count == q), i, chosen[q]) for q in range(MOST)
        ]
        count = count + here.astype(jnp.int32)
    load_sub.wait()
    for t in range(MOST):
        for ri in range(2):
            block = sub_ref[ri, chosen[t]]
            for h in range(2):
                seg[t, h, ri, f] = block[:, h * HALF : (h + 1) * HALF]

    pl.semaphore_wait(barrier, OWNERS + 1)

    def ring_ref(way, c, step, origin):
        t, h, n = CHUNKS[c]
        part = seg.at[t, pl.ds(h, n)]
        return part.at[:, :, origin] if step < 4 else part.at[:, way, origin]

    def piece(way, c, step):
        if way == 0:
            origin, target = lax.rem(f + FAC - (step - 1), FAC), right
        else:
            origin, target = lax.rem(f + step - 1, FAC), left
        ref = ring_ref(way, c, step, origin)
        return pltpu.make_async_remote_copy(
            src_ref=ref,
            dst_ref=ref,
            send_sem=ring_send.at[way, c, step - 1],
            recv_sem=ring_recv.at[way, c, step - 1],
            device_id=(s, target),
            device_id_type=MESH,
        )

    def arrived(way, c, step):
        if way == 0:
            origin = lax.rem(f + FAC - step, FAC)
        else:
            origin = lax.rem(f + step, FAC)
        ref = ring_ref(way, c, step, origin)
        pltpu.make_async_copy(ref, ref, ring_recv.at[way, c, step - 1]).wait()

    def issue(c, step):
        for way in range(2):
            if step > 1:
                arrived(way, c, step - 1)
            piece(way, c, step).start()

    def tables():
        load_base.wait()
        pixel = lax.broadcasted_iota(jnp.int32, (1, XA), 1)

        def centred(centre):
            cosine, sine = phases(centre, pixel)
            return cosine * base[0] - sine * base[1], cosine * base[1] + sine * base[0]

        parts = [part.reshape(OWNERS, ROWS, XA) for part in centred(centre_ref[0, f // 2])]
        for first, part in ((0, parts), (XA, (-parts[1], parts[0]))):
            row_table[:, first : first + XA] = (
                jnp.concatenate(part, axis=1).reshape(2 * XMYN, XA).astype(jnp.bfloat16)
            )
        for v in range(2):
            for ri, part in enumerate(centred(centre_ref[1, lax.rem(f, 2) * 2 + v])):
                first = (v * 2 + ri) * XMYN
                col_table[first : first + XMYN, :] = part.astype(jnp.bfloat16)
        places()

    def places():
        load_cov.wait()
        load_off.wait()
        slots = OWNERS * SLOT_DEV
        here = cov_vec[0:1, :]
        row = lax.broadcasted_iota(jnp.int32, (slots, slots), 0)
        col = lax.broadcasted_iota(jnp.int32, (slots, slots), 1)
        before = jnp.logical_and(row // SLOT_DEV == col // SLOT_DEV, col < row)
        lhs = jnp.broadcast_to(here, (8, slots)).astype(jnp.bfloat16)
        nt = (((1,), (1,)), ((), ()))
        rank = lax.dot_general(
            lhs, before.astype(jnp.bfloat16), nt, preferred_element_type=jnp.float32
        )
        owner = lax.broadcasted_iota(jnp.int32, (8, slots), 1) // SLOT_DEV
        source = shifted(owner, s, -1)
        code = (rank * OWNERS + source.astype(jnp.float32) + 1.0) * lhs.astype(jnp.float32)
        target = off_vec[0:1, :] * VGRID + off_vec[1:2, :]
        hit = (row == target).astype(jnp.bfloat16)
        found = lax.dot_general(
            code.astype(jnp.bfloat16), hit, nt, preferred_element_type=jnp.float32
        )
        index = found.astype(jnp.int32) - 1
        where_ref[...] = jnp.where(index < 0, MOST * OWNERS, index)
        pieces_ref[MOST * OWNERS] = jnp.zeros((8, ROWS, VGRID), jnp.float32)

    def swap_copy(c, d):
        t, h, n = SWAPS[c]
        target, back = shifted(s, d), shifted(0, d, -1)
        return pltpu.make_async_remote_copy(
            src_ref=half.at[t, pl.ds(h, n), target],
            dst_ref=recv.at[t, pl.ds(h, n), back],
            send_sem=swap_send.at[c],
            recv_sem=swap_recv.at[c],
            device_id=(target, f),
            device_id_type=MESH,
        )

    def row_pass(c):
        t, first, n = CHUNKS[c]
        for way in range(2):
            arrived(way, c, 4)
        for h in range(first, first + n):
            block = seg[t, h].reshape(2 * XA, HALF)
            product = jnp.dot(row_table[...], block, preferred_element_type=jnp.float32)
            half[t, h] = product.astype(jnp.bfloat16).reshape(OWNERS, 2 * ROWS, HALF)

        for d in FARTHEST if c in SWAPS else ():
            swap_copy(c, d).start()

        for h in range(first, first + n):
            recv[t, h, 0] = half[t, h, s]

    def column_pass(c):
        t, first, n = SWAPS[c]
        whole = recv.at[t, pl.ds(first, n), pl.ds(1, OWNERS - 1)]
        pltpu.make_async_copy(whole, whole, swap_recv.at[c]).wait()
        for v in range(2):
            product = []
            for ri in range(2):
                rows = slice((v * 2 + ri) * XMYN, (v * 2 + ri + 1) * XMYN)
                total = None
                for h in range(first, first + n):
                    term = lax.dot_general(
                        recv[t, h].reshape(OWNERS * 2 * ROWS, HALF),
                        col_table[rows, h * HALF : (h + 1) * HALF],
                        (((1,), (1,)), ((), ())),
                        preferred_element_type=jnp.float32,
                    )
                    total = term if total is None else total + term
                product.append(total.reshape(OWNERS, 2, ROWS, XMYN))
            real = product[0][:, 0] - product[1][:, 1]
            imag = product[1][:, 0] + product[0][:, 1]
            for ri, value in enumerate((real, imag)):
                for part in range(2):
                    tile = value[:, :, part * VGRID : (part + 1) * VGRID]
                    k = (ri * 2 + v) * 2 + part
                    if first > 0:
                        tile = tile + pieces_ref[t * OWNERS : (t + 1) * OWNERS, k]
                    pieces_ref[t * OWNERS : (t + 1) * OWNERS, k] = tile

    def ring_sent():
        for c in range(len(CHUNKS)):
            for step in range(1, 5):
                for way in range(2):
                    piece(way, c, step).wait_send()

    for entry in SCHEDULE:
        if entry == "T":
            tables()
        elif entry == "W":
            ring_sent()
        elif isinstance(entry, tuple):
            issue(*entry)
        elif entry[0] == "F":
            row_pass(int(entry[1:]))
        else:
            column_pass(int(entry[1:]))

    for c, (t, first, n) in SWAPS.items():
        whole = half.at[t, pl.ds(first, n), pl.ds(1, OWNERS - 1)]
        pltpu.make_async_copy(whole, whole, swap_send.at[c]).wait()


def place_kernel(where_ref, pieces_ref, out_hbm, strips, out_sem):
    stores = []
    span = VGRID // SECTIONS
    for c in range(COLS):

        def at(p, c=c):
            return where_ref[0, c * VGRID + (p & (VGRID - 1))]

        def body(i, here, at=at, c=c):
            sums = []
            for step in range(GROUP):
                after = at(i * GROUP + step + 1)
                for k in range(4):
                    sums.append(pieces_ref[here, 2 * k + 1] + pieces_ref[after, 2 * k])
                here = after
            for step in range(GROUP):
                start = (i * GROUP + step) * VGRID
                lanes = pl.ds(pl.multiple_of(start, VGRID), VGRID)
                for k in range(4):
                    strips[k, c, :, lanes] = sums[step * 4 + k]
            return here

        here = at(0)
        for q in range(SECTIONS):
            first, last = q * span // GROUP, (q + 1) * span // GROUP
            here = lax.fori_loop(first, last, body, here, unroll=2)
            lanes = pl.ds(q * span * VGRID, span * VGRID)
            for k in range(4):
                store = pltpu.make_async_copy(
                    strips.at[k, c, :, lanes],
                    out_hbm.at[k // 2, c, k % 2, :, lanes],
                    out_sem.at[k, c, q],
                )
                store.start()
                stores.append(store)
    for store in stores:
        store.wait()


def local(subgrids, sub_offsets, coverage, facet_offsets):
    base = constants()
    smem = pl.BlockSpec(memory_space=pltpu.SMEM)
    vmem = pl.BlockSpec(memory_space=pltpu.VMEM)
    hbm = pl.BlockSpec(memory_space=pltpu.HBM)
    anywhere = pl.BlockSpec(memory_space=pl.ANY)
    bf16, f32 = jnp.bfloat16, jnp.float32
    dma = pltpu.SemaphoreType.DMA
    hb = lambda x: pltpu.with_memory_space_constraint(x, pltpu.HBM)
    slots = OWNERS * SLOT_DEV
    chunks = len(CHUNKS)
    pieces, where = pl.pallas_call(
        exchange_kernel,
        out_shape=[
            jax.ShapeDtypeStruct((MOST * OWNERS + 1, 8, ROWS, VGRID), f32),
            jax.ShapeDtypeStruct((8, slots), jnp.int32),
        ],
        in_specs=[smem, smem, hbm, hbm, hbm, hbm],
        out_specs=[vmem, vmem],
        scratch_shapes=[
            pltpu.VMEM((1, slots), jnp.int32),
            pltpu.VMEM((2, slots), jnp.int32),
            pltpu.VMEM((2, SLOT_DEV, XB, XA), bf16),
            pltpu.VMEM((MOST, 2, 2, FAC, XB, HALF), bf16),
            pltpu.VMEM((2 * XMYN, 2 * XA), bf16),
            pltpu.VMEM((4 * XMYN, XA), bf16),
            pltpu.VMEM((MOST, 2, OWNERS, 2 * ROWS, HALF), bf16),
            pltpu.VMEM((MOST, 2, OWNERS, 2 * ROWS, HALF), bf16),
            pltpu.VMEM((2, XMYN, XA), f32),
            dma((2, chunks, 4)),
            dma((2, chunks, 4)),
            dma((chunks,)),
            dma((chunks,)),
            dma((4,)),
        ],
        compiler_params=pltpu.CompilerParams(
            collective_id=0, has_side_effects=True, vmem_limit_bytes=40 * 2**20
        ),
        name="exchange",
    )(
        hb(coverage),
        hb(facet_offsets),
        hb(coverage.reshape(1, slots)),
        hb(sub_offsets.T),
        hb(subgrids),
        hb(jnp.asarray(base)),
    )
    return pl.pallas_call(
        place_kernel,
        out_shape=jax.ShapeDtypeStruct((2, COLS, 2, ROWS, YN), f32),
        in_specs=[smem, vmem],
        out_specs=anywhere,
        scratch_shapes=[
            pltpu.VMEM((4, COLS, ROWS, YN), f32),
            dma((4, COLS, SECTIONS)),
        ],
        compiler_params=pltpu.CompilerParams(vmem_limit_bytes=40 * 2**20),
        name="place",
    )(where, pieces)


def solution(mesh):
    placed = (P(None, "sub", "fac", None), P(), P(), P())
    return jax.shard_map(
        local,
        mesh=mesh,
        in_specs=placed,
        out_specs=P(None, None, "fac", "sub", None),
        check_vma=False,
    )
```

```python
import functools
import math

import jax
import jax.numpy as jnp
import numpy as np
from jax import lax
from jax.experimental import pallas as pl
from jax.experimental.pallas import tpu as pltpu
from jax.sharding import PartitionSpec as P

XA = 512
XMYN = 256
VGRID = 128
FROWS = 4
COLS = 2
XM = 1024
YN = 16384
SLOT_DEV = 8
MOST = 4
OWNERS = 32
FAC = 8
XB = XA // FAC
ROWS = XMYN // OWNERS
TAPER = 0.6
SECTIONS = 8
GROUP = 8

MESH = pl.DeviceIdType.MESH

HALF = XA // 2

CHUNKS = ((0, 0, 1), (0, 1, 1), (1, 0, 1), (1, 1, 1), (2, 0, 1), (2, 1, 1), (3, 0, 1), (3, 1, 1))

SCHEDULE = (
    (0, 1), (1, 1), (2, 1), "T", (3, 1), (0, 2), (1, 2), (2, 2), (3, 2), (0, 3), (1, 3), (2, 3),
    (4, 1), (0, 4), (1, 4), (5, 1), (3, 3), (2, 4), "F0", (4, 2), "F1", (3, 4), (6, 1), (5, 2),
    "F2", (4, 3), (7, 1), (5, 3), "F3", (6, 2), (4, 4), (7, 2), (5, 4), (6, 3), "F4", (7, 3),
    "F5", (6, 4), (7, 4), "F6", "F7", "G0", "G1", "G2", "G3", "W", "G4", "G5",
    "G6", "G7",
)


def base_table():
    h = XMYN // 2
    k = np.arange(XMYN) - h
    x = np.arange(XA) - XA // 2
    kernel = np.exp(-2j * np.pi / XMYN * np.mod(k[:, None] * k[None, :], XMYN))
    taper = np.exp(-0.5 * (k / (TAPER * h)) ** 2)
    wave = np.exp(2j * np.pi / XM * np.mod(k[:, None] * x[None, :], XM))
    return kernel @ (taper[:, None] * wave) / math.sqrt(XMYN * XA)


def constants():
    table = base_table()
    real = table.real.astype(np.float32)
    imag = table.imag.astype(np.float32)

    return np.stack([real, imag])


def phases(centre, pixel):
    index = (centre * (pixel - XA // 2)) & (XM - 1)
    angle = (2.0 * math.pi / XM) * index.astype(jnp.float32)
    return jnp.cos(angle), jnp.sin(angle)


def shifted(index, by, sign=1):
    x = ((index >> 3) + sign * (by >> 3)) & 3
    y = ((index >> 1 & 3) + sign * (by >> 1 & 3)) & 3
    return x * 8 + y * 2 + ((index ^ by) & 1)


def hops(by):
    x, y = by >> 3, by >> 1 & 3
    return min(x, 4 - x) + min(y, 4 - y)


FARTHEST = sorted(range(1, OWNERS), key=lambda by: -hops(by))


def exchange_kernel(
    cov_ref,
    centre_ref,
    cov_hbm,
    off_hbm,
    sub_hbm,
    base_hbm,
    pieces_ref,
    where_ref,
    cov_vec,
    off_vec,
    sub_ref,
    seg,
    row_table,
    col_table,
    half,
    recv,
    base,
    ring_send,
    ring_recv,
    swap_send,
    swap_recv,
    load_sem,
):
    s = lax.axis_index("sub")
    f = lax.axis_index("fac")
    right = lax.rem(f + 1, FAC)
    left = lax.rem(f + FAC - 1, FAC)

    load_sub = pltpu.make_async_copy(sub_hbm, sub_ref, load_sem.at[0])
    load_base = pltpu.make_async_copy(base_hbm, base, load_sem.at[1])
    load_cov = pltpu.make_async_copy(cov_hbm, cov_vec, load_sem.at[2])
    load_off = pltpu.make_async_copy(off_hbm, off_vec, load_sem.at[3])
    for load in (load_sub, load_base, load_cov, load_off):
        load.start()

    barrier = pltpu.get_barrier_semaphore()
    for neighbour in (left, right):
        pl.semaphore_signal(barrier, inc=1, device_id=(s, neighbour), device_id_type=MESH)

    for d in range(1, OWNERS):
        pl.semaphore_signal(
            barrier, inc=1, device_id=(lax.rem(s + d, OWNERS), f), device_id_type=MESH
        )

    chosen = [jnp.int32(0)] * MOST
    count = jnp.int32(0)
    for i in range(SLOT_DEV):
        here = cov_ref[s * SLOT_DEV + i] > 0
        chosen = [
            jnp.where(jnp.logical_and(here, count == q), i, chosen[q]) for q in range(MOST)
        ]
        count = count + here.astype(jnp.int32)
    load_sub.wait()
    for t in range(MOST):
        for ri in range(2):
            block = sub_ref[ri, chosen[t]]
            for h in range(2):
                seg[t, h, ri, f] = block[:, h * HALF : (h + 1) * HALF]

    pl.semaphore_wait(barrier, OWNERS + 1)

    def ring_ref(way, c, step, origin):
        t, h, n = CHUNKS[c]
        part = seg.at[t, pl.ds(h, n)]
        return part.at[:, :, origin] if step < 4 else part.at[:, way, origin]

    def piece(way, c, step):
        if way == 0:
            origin, target = lax.rem(f + FAC - (step - 1), FAC), right
        else:
            origin, target = lax.rem(f + step - 1, FAC), left
        ref = ring_ref(way, c, step, origin)
        return pltpu.make_async_remote_copy(
            src_ref=ref,
            dst_ref=ref,
            send_sem=ring_send.at[way, c, step - 1],
            recv_sem=ring_recv.at[way, c, step - 1],
            device_id=(s, target),
            device_id_type=MESH,
        )

    def arrived(way, c, step):
        if way == 0:
            origin = lax.rem(f + FAC - step, FAC)
        else:
            origin = lax.rem(f + step, FAC)
        ref = ring_ref(way, c, step, origin)
        pltpu.make_async_copy(ref, ref, ring_recv.at[way, c, step - 1]).wait()

    def issue(c, step):
        for way in range(2):
            if step > 1:
                arrived(way, c, step - 1)
            piece(way, c, step).start()

    def tables():
        load_base.wait()
        pixel = lax.broadcasted_iota(jnp.int32, (1, XA), 1)

        def centred(centre):
            cosine, sine = phases(centre, pixel)
            return cosine * base[0] - sine * base[1], cosine * base[1] + sine * base[0]

        parts = [part.reshape(OWNERS, ROWS, XA) for part in centred(centre_ref[0, f // 2])]
        for first, part in ((0, parts), (XA, (-parts[1], parts[0]))):
            row_table[:, first : first + XA] = (
                jnp.concatenate(part, axis=1).reshape(2 * XMYN, XA).astype(jnp.bfloat16)
            )
        for v in range(2):
            for ri, part in enumerate(centred(centre_ref[1, lax.rem(f, 2) * 2 + v])):
                first = (v * 2 + ri) * XMYN
                col_table[first : first + XMYN, :] = part.astype(jnp.bfloat16)
        places()

    def places():
        load_cov.wait()
        load_off.wait()
        slots = OWNERS * SLOT_DEV
        here = cov_vec[0:1, :]
        row = lax.broadcasted_iota(jnp.int32, (slots, slots), 0)
        col = lax.broadcasted_iota(jnp.int32, (slots, slots), 1)
        before = jnp.logical_and(row // SLOT_DEV == col // SLOT_DEV, col < row)
        lhs = jnp.broadcast_to(here, (8, slots)).astype(jnp.bfloat16)
        nt = (((1,), (1,)), ((), ()))
        rank = lax.dot_general(
            lhs, before.astype(jnp.bfloat16), nt, preferred_element_type=jnp.float32
        )
        owner = lax.broadcasted_iota(jnp.int32, (8, slots), 1) // SLOT_DEV
        source = shifted(owner, s, -1)
        code = (rank * OWNERS + source.astype(jnp.float32) + 1.0) * lhs.astype(jnp.float32)
        target = off_vec[0:1, :] * VGRID + off_vec[1:2, :]
        hit = (row == target).astype(jnp.bfloat16)
        found = lax.dot_general(
            code.astype(jnp.bfloat16), hit, nt, preferred_element_type=jnp.float32
        )
        index = found.astype(jnp.int32) - 1
        where_ref[...] = jnp.where(index < 0, MOST * OWNERS, index)
        pieces_ref[MOST * OWNERS] = jnp.zeros((8, ROWS, VGRID), jnp.float32)

    def swap_copy(c, d):
        t, h, n = CHUNKS[c]
        target, back = shifted(s, d), shifted(0, d, -1)
        return pltpu.make_async_remote_copy(
            src_ref=half.at[t, pl.ds(h, n), target],
            dst_ref=recv.at[t, pl.ds(h, n), back],
            send_sem=swap_send.at[c],
            recv_sem=swap_recv.at[c],
            device_id=(target, f),
            device_id_type=MESH,
        )

    def row_pass(c):
        t, first, n = CHUNKS[c]
        for way in range(2):
            arrived(way, c, 4)
        for h in range(first, first + n):
            block = seg[t, h].reshape(2 * XA, HALF)
            product = jnp.dot(row_table[...], block, preferred_element_type=jnp.float32)
            half[t, h] = product.astype(jnp.bfloat16).reshape(OWNERS, 2 * ROWS, HALF)

        for d in FARTHEST:
            swap_copy(c, d).start()

        for h in range(first, first + n):
            recv[t, h, 0] = half[t, h, s]

    def column_pass(c):
        t, first, n = CHUNKS[c]
        whole = recv.at[t, pl.ds(first, n), pl.ds(1, OWNERS - 1)]
        pltpu.make_async_copy(whole, whole, swap_recv.at[c]).wait()
        for v in range(2):
            product = []
            for ri in range(2):
                rows = slice((v * 2 + ri) * XMYN, (v * 2 + ri + 1) * XMYN)
                total = None
                for h in range(first, first + n):
                    term = lax.dot_general(
                        recv[t, h].reshape(OWNERS * 2 * ROWS, HALF),
                        col_table[rows, h * HALF : (h + 1) * HALF],
                        (((1,), (1,)), ((), ())),
                        preferred_element_type=jnp.float32,
                    )
                    total = term if total is None else total + term
                product.append(total.reshape(OWNERS, 2, ROWS, XMYN))
            real = product[0][:, 0] - product[1][:, 1]
            imag = product[1][:, 0] + product[0][:, 1]
            for ri, value in enumerate((real, imag)):
                for part in range(2):
                    tile = value[:, :, part * VGRID : (part + 1) * VGRID]
                    k = (ri * 2 + v) * 2 + part
                    if first > 0:
                        tile = tile + pieces_ref[t * OWNERS : (t + 1) * OWNERS, k]
                    pieces_ref[t * OWNERS : (t + 1) * OWNERS, k] = tile

    def ring_sent():
        for c in range(len(CHUNKS)):
            for step in range(1, 5):
                for way in range(2):
                    piece(way, c, step).wait_send()

    for entry in SCHEDULE:
        if entry == "T":
            tables()
        elif entry == "W":
            ring_sent()
        elif isinstance(entry, tuple):
            issue(*entry)
        elif entry[0] == "F":
            row_pass(int(entry[1:]))
        else:
            column_pass(int(entry[1:]))

    for c, (t, first, n) in enumerate(CHUNKS):
        whole = half.at[t, pl.ds(first, n), pl.ds(1, OWNERS - 1)]
        pltpu.make_async_copy(whole, whole, swap_send.at[c]).wait()


def place_kernel(where_ref, pieces_ref, out_hbm, strips, out_sem):
    stores = []
    span = VGRID // SECTIONS
    for c in range(COLS):

        def at(p, c=c):
            return where_ref[0, c * VGRID + (p & (VGRID - 1))]

        def body(i, here, at=at, c=c):
            sums = []
            for step in range(GROUP):
                after = at(i * GROUP + step + 1)
                for k in range(4):
                    sums.append(pieces_ref[here, 2 * k + 1] + pieces_ref[after, 2 * k])
                here = after
            for step in range(GROUP):
                start = (i * GROUP + step) * VGRID
                lanes = pl.ds(pl.multiple_of(start, VGRID), VGRID)
                for k in range(4):
                    strips[k, c, :, lanes] = sums[step * 4 + k]
            return here

        here = at(0)
        for q in range(SECTIONS):
            first, last = q * span // GROUP, (q + 1) * span // GROUP
            here = lax.fori_loop(first, last, body, here, unroll=2)
            lanes = pl.ds(q * span * VGRID, span * VGRID)
            for k in range(4):
                store = pltpu.make_async_copy(
                    strips.at[k, c, :, lanes],
                    out_hbm.at[k // 2, c, k % 2, :, lanes],
                    out_sem.at[k, c, q],
                )
                store.start()
                stores.append(store)
    for store in stores:
        store.wait()


def local(subgrids, sub_offsets, coverage, facet_offsets):
    base = constants()
    smem = pl.BlockSpec(memory_space=pltpu.SMEM)
    vmem = pl.BlockSpec(memory_space=pltpu.VMEM)
    hbm = pl.BlockSpec(memory_space=pltpu.HBM)
    anywhere = pl.BlockSpec(memory_space=pl.ANY)
    bf16, f32 = jnp.bfloat16, jnp.float32
    dma = pltpu.SemaphoreType.DMA
    hb = lambda x: pltpu.with_memory_space_constraint(x, pltpu.HBM)
    slots = OWNERS * SLOT_DEV
    chunks = len(CHUNKS)
    pieces, where = pl.pallas_call(
        exchange_kernel,
        out_shape=[
            jax.ShapeDtypeStruct((MOST * OWNERS + 1, 8, ROWS, VGRID), f32),
            jax.ShapeDtypeStruct((8, slots), jnp.int32),
        ],
        in_specs=[smem, smem, hbm, hbm, hbm, hbm],
        out_specs=[vmem, vmem],
        scratch_shapes=[
            pltpu.VMEM((1, slots), jnp.int32),
            pltpu.VMEM((2, slots), jnp.int32),
            pltpu.VMEM((2, SLOT_DEV, XB, XA), bf16),
            pltpu.VMEM((MOST, 2, 2, FAC, XB, HALF), bf16),
            pltpu.VMEM((2 * XMYN, 2 * XA), bf16),
            pltpu.VMEM((4 * XMYN, XA), bf16),
            pltpu.VMEM((MOST, 2, OWNERS, 2 * ROWS, HALF), bf16),
            pltpu.VMEM((MOST, 2, OWNERS, 2 * ROWS, HALF), bf16),
            pltpu.VMEM((2, XMYN, XA), f32),
            dma((2, chunks, 4)),
            dma((2, chunks, 4)),
            dma((chunks,)),
            dma((chunks,)),
            dma((4,)),
        ],
        compiler_params=pltpu.CompilerParams(
            collective_id=0, has_side_effects=True, vmem_limit_bytes=40 * 2**20
        ),
        name="exchange",
    )(
        hb(coverage),
        hb(facet_offsets),
        hb(coverage.reshape(1, slots)),
        hb(sub_offsets.T),
        hb(subgrids),
        hb(jnp.asarray(base)),
    )
    return pl.pallas_call(
        place_kernel,
        out_shape=jax.ShapeDtypeStruct((2, COLS, 2, ROWS, YN), f32),
        in_specs=[smem, vmem],
        out_specs=anywhere,
        scratch_shapes=[
            pltpu.VMEM((4, COLS, ROWS, YN), f32),
            dma((4, COLS, SECTIONS)),
        ],
        compiler_params=pltpu.CompilerParams(vmem_limit_bytes=40 * 2**20),
        name="place",
    )(where, pieces)


def solution(mesh):
    placed = (P(None, "sub", "fac", None), P(), P(), P())
    return jax.shard_map(
        local,
        mesh=mesh,
        in_specs=placed,
        out_specs=P(None, None, "fac", "sub", None),
        check_vma=False,
    )
```
